256 devices in a mesh: seq: 2 (over core), row: 8 (over x, z_hi), col: 16 (over z_lo, y).
Axes of the slice: x: 4, y: 4, z: 8 (z_hi: 2, z_lo: 4; z = z_hi * 4 + z_lo), core: 2. Of those that a mesh axis runs over, the one named last changes fastest.
Arguments:
- first_linear_features: bfloat16 [256, 1536, 32], P('seq', ('row', 'col')), may hold values from -10 to 10
- second_linear_features: bfloat16 [256, 1536, 32], P('seq', ('col', 'row')), may hold values from -10 to 10
- coverage_indicator: int32 [256, 1536], replicated, may hold values from 0 to 1, as said below
- final_linear_matrix: bfloat16 [1024, 128], replicated, may hold values from -0.1875 to 0.1875
- final_offset_vector: float32 [128], replicated, may hold values from -6 to 6
Outputs:
- pair_delta_update: bfloat16 [1536, 1536, 128], P('row', ('col', 'seq'))
The draws below stay inside these ranges and needn't reach their ends.
Inputs may be any that keep to these rules, and one draw needn't show every extreme that they name: `coverage_indicator`: each entry is 0 or 1; some residues are masked in every sequence.
All inputs are finite; a program needn't handle non-finite values.
Results may differ from the reference program's by a relative error of at most 0.0044.
Values may be sent and summed in bfloat16 or wider, within the bound.
A program may use at most 128 MiB of HBM per device.

```python
import jax
import jax.numpy as jnp
from jax import lax

FACTOR_CHANNELS = 32
CZ = 128
HOMOLOG_COUNT = 256
SB = 128
CHAIN_LENGTH = 1536


def draw_coverage_indicator(key, part):
    key = jax.random.fold_in(key, 7)
    level_key, value_key = jax.random.split(key)
    levels = jax.random.randint(level_key, (1, CHAIN_LENGTH), 0, 9)
    values = jax.random.randint(value_key, (HOMOLOG_COUNT, CHAIN_LENGTH), 0, 24)
    ranks = jnp.arange(HOMOLOG_COUNT, dtype=jnp.int32)[:, None]
    factor = 1 + 2 * (2 * ranks // HOMOLOG_COUNT)
    return (values < levels * factor).astype(jnp.int32)


def shard_levels(key, shape, pieces, smallest, largest):
    def one(dim, parts):
        steps = jax.random.uniform(jax.random.fold_in(jax.random.fold_in(key, 6), dim), (parts,), jnp.float32, smallest / len(pieces), largest / len(pieces))
        return jnp.repeat(jnp.exp(steps), shape[dim] // parts).reshape((-1,) + (1,) * (len(shape) - dim - 1))

    gain = one(*pieces[0])
    for cut in pieces[1:]:
        gain = gain * one(*cut)
    return gain


def scatter_about(key, dims, spread, reach, shards=(), kind=jnp.bfloat16):
    level = shard_levels(key, dims, shards, -0.22, 0.18) if shards else 1.0
    entries = jax.random.normal(key, dims, jnp.float32) * spread * level
    return jnp.minimum(jnp.maximum(entries, -reach), reach).astype(kind)


def setup_inputs(seed: int = 0) -> dict:
    seeds = jax.random.split(jax.random.key(seed), 6)
    first_linear_features = scatter_about(seeds[0], (HOMOLOG_COUNT, CHAIN_LENGTH, FACTOR_CHANNELS), 2.0, 10.0, ((0, 2), (1, 128)))
    second_linear_features = scatter_about(seeds[1], (HOMOLOG_COUNT, CHAIN_LENGTH, FACTOR_CHANNELS), 2.0, 10.0, ((0, 2), (1, 128)))
    coverage_indicator = draw_coverage_indicator(jax.random.fold_in(seeds[5], 71), 0)
    final_linear_matrix = scatter_about(seeds[3], (FACTOR_CHANNELS * FACTOR_CHANNELS, CZ), (FACTOR_CHANNELS * FACTOR_CHANNELS) ** -0.5, 0.1875)
    final_offset_vector = scatter_about(seeds[4], (CZ,), 1.0, 6.0, (), jnp.float32)
    return {"first_linear_features": first_linear_features, "second_linear_features": second_linear_features, "coverage_indicator": coverage_indicator, "final_linear_matrix": final_linear_matrix, "final_offset_vector": final_offset_vector}


def pair_rows(a_block, b_block, final_linear_matrix):
    seq_count, row_count, chan_count = a_block.shape
    col_count = b_block.shape[1]
    product = lax.dot_general(a_block.reshape(seq_count, row_count * chan_count), b_block.reshape(seq_count, col_count * chan_count), (((0,), (0,)), ((), ())), preferred_element_type=jnp.float32)
    product = product.reshape(row_count, chan_count, col_count, chan_count).transpose(0, 2, 1, 3)
    product = product.reshape(row_count * col_count, chan_count * chan_count).astype(jnp.bfloat16)
    return jnp.dot(product, final_linear_matrix, preferred_element_type=jnp.float32).reshape(row_count, col_count, final_linear_matrix.shape[1])


def project_pairs(first_factor_zeroed, second_factor_zeroed, final_linear_matrix, seq_block, row_step):
    seq_total, row_count, chan_count = first_factor_zeroed.shape
    col_count = second_factor_zeroed.shape[1]
    running = jnp.zeros((row_count, col_count, final_linear_matrix.shape[1]), jnp.float32)
    for offset in range(0, seq_total, seq_block):
        a_part = first_factor_zeroed[offset:offset + seq_block]
        b_part = second_factor_zeroed[offset:offset + seq_block]

        def one_slab(slab_index):
            a_slab = lax.dynamic_slice_in_dim(a_part, slab_index * row_step, row_step, 1)
            return pair_rows(a_slab, b_part, final_linear_matrix)

        slab_out = lax.map(one_slab, jnp.arange(row_count // row_step, dtype=jnp.int32))
        running = running + slab_out.reshape(row_count, col_count, final_linear_matrix.shape[1])
    return running


def reference(first_linear_features, second_linear_features, coverage_indicator, final_linear_matrix, final_offset_vector):
    coverage_flags = coverage_indicator.astype(jnp.bfloat16)
    first_factor_zeroed = first_linear_features * coverage_flags[:, :, None]
    second_factor_zeroed = second_linear_features * coverage_flags[:, :, None]
    summed = project_pairs(first_factor_zeroed, second_factor_zeroed, final_linear_matrix, SB, 16)
    counts = lax.dot_general(coverage_flags, coverage_flags, (((0,), (0,)), ((), ())), preferred_element_type=jnp.float32)
    return ((summed + final_offset_vector) / jnp.maximum(counts, 1.0)[:, :, None]).astype(jnp.bfloat16)
```

```python
import functools

import jax
import jax.numpy as jnp
from jax import lax
from jax.experimental import pallas as pl
from jax.experimental.pallas import tpu as pltpu
from jax.sharding import PartitionSpec as P

MESH = pl.DeviceIdType.MESH
F32 = jnp.float32
BF16 = jnp.bfloat16

CHAN = 32
BLK = 12
ROWS = BLK * CHAN
LANES = 128
NJ = 48
SLAB = 48
CZ = 128


def when_all(*conds):
    c = conds[0]
    for d in conds[1:]:
        c = jnp.logical_and(c, d)
    return pl.when(c)


def kernel(
    a_hbm, b_hbm, m_hbm, w_hbm, bias_ref, o_hbm,
    a_all, b_all, a_own, b_own, b_far, m_i, m_j, mt_i, mt_j, w_in, f_tmp, b_rot, w_rot, pairs, rcs, o_buf,
    load_sem, out_sem,
    bsend, brecv, fsend, frecv, zsend, zrecv, ysend, yrecv, csend, crecv,
):
    k = lax.axis_index("seq")
    row = lax.axis_index("row")
    col = lax.axis_index("col")
    x, zh = row // 2, row % 2
    zl, y = col // 4, col % 4
    half = x // 2
    yp, ym = (y + 1) % 4, (y + 3) % 4

    i_first = row * 192
    j_first = col * 96
    i_win = pl.multiple_of((i_first // 128) * 128, 128)
    j_win = pl.multiple_of(jnp.minimum((j_first // 128) * 128, 1280), 128)
    loads = [
        pltpu.make_async_copy(m_hbm.at[:, pl.ds(i_win, 256)], m_i, load_sem.at[0]),
        pltpu.make_async_copy(m_hbm.at[:, pl.ds(j_win, 256)], m_j, load_sem.at[1]),
        pltpu.make_async_copy(a_hbm, a_own, load_sem.at[2]),
        pltpu.make_async_copy(b_hbm, b_own, load_sem.at[3]),
        pltpu.make_async_copy(w_hbm, w_in, load_sem.at[4]),
    ]
    for c in loads:
        c.start()

    barrier = pltpu.get_barrier_semaphore()
    peers = [(1 - k, row, col), (k, row ^ 1, col)]
    for dx in (1, 2, 3):
        peers += [(s, row ^ (2 * dx), col) for s in (0, 1)]
    peers += [(k, row, col ^ (4 * g)) for g in (1, 2, 3)]
    peers += [(k, row, zl * 4 + yp), (k, row, zl * 4 + ym)]
    for p in peers:
        pl.semaphore_signal(barrier, inc=1, device_id=p, device_id_type=MESH)

    loads[0].wait()
    for s in range(2):
        mt_i[s] = m_i[pl.ds(s * LANES, LANES), :].astype(F32).T
    loads[1].wait()
    for s in range(2):
        mt_j[s] = m_j[pl.ds(s * LANES, LANES), :].astype(F32).T
    loads[3].wait()
    jo = j_first + row * BLK - j_win
    for n in range(BLK):
        flags = mt_j[k, pl.ds(jo + n, 1), :].astype(BF16)
        sl = pl.ds(n * CHAN, CHAN)
        b_own[sl, :] = b_own[sl, :] * flags
    loads[2].wait()
    io = i_first + col * BLK - i_win
    for n in range(BLK):
        flags = mt_i[k, pl.ds(io + n, 1), :].astype(BF16)
        sl = pl.ds(n * CHAN, CHAN)
        a_all[col, k, sl, :] = a_own[sl, :] * flags

    pl.semaphore_wait(barrier, len(peers))

    HALF = ROWS // 2
    far = [
        pltpu.make_async_remote_copy(
            src_ref=b_own.at[pl.ds(h * HALF, HALF)],
            dst_ref=b_far.at[pl.ds(h * HALF, HALF)],
            send_sem=fsend.at[h],
            recv_sem=frecv.at[h],
            device_id=(k, row ^ 1, col),
            device_id_type=MESH,
        )
        for h in range(2)
    ]

    def b_copy(origin, h, dx):
        src = (b_own, b_far)[origin].at[pl.ds(h * HALF, HALF)]
        slot = (x % 2) * 2 + (zh if origin == 0 else 1 - zh)
        dst = b_all.at[slot, k, pl.ds(h * HALF, HALF)]
        return src, dst, brecv.at[slot, k, h]

    def b_spread(origin, h):
        for dx in (1, 3, 2):
            src, dst, sem = b_copy(origin, h, dx)
            pltpu.make_async_remote_copy(
                src_ref=src, dst_ref=dst, send_sem=bsend.at[origin, h, dx], recv_sem=sem,
                device_id=(half, row ^ (2 * dx), col), device_id_type=MESH,
            ).start()
        src, dst, sem = b_copy(origin, h, 0)

        @pl.when(half == k)
        def _():
            pltpu.make_async_copy(src, dst, sem).start()

        @pl.when(half != k)
        def _():
            pltpu.make_async_remote_copy(
                src_ref=src, dst_ref=dst, send_sem=bsend.at[origin, h, 0], recv_sem=sem,
                device_id=(1 - k, row, col), device_id_type=MESH,
            ).start()

    def b_drain():
        for origin in range(2):
            for h in range(2):
                for dx in range(4):
                    src, dst, sem = b_copy(origin, h, dx)

                    def done():
                        pltpu.make_async_copy(src, src, bsend.at[origin, h, dx]).wait()

                    if dx:
                        done()
                    else:
                        pl.when(half != k)(done)

    PIECES = ((0, ROWS), (0, ROWS), (0, ROWS), (0, HALF), (HALF, HALF))

    def a_piece(g, role, core):
        zg = zl ^ g
        yy = (y, ym, yp, (y + 2) % 4, (y + 2) % 4)[role]
        first, size = PIECES[role]
        return a_all.at[zg * 4 + yy, core, pl.ds(first, size)]

    def to_core(g, role):
        piece = a_piece(g, role, k)
        return pltpu.make_async_remote_copy(
            src_ref=piece, dst_ref=piece, send_sem=csend.at[g, role], recv_sem=crecv.at[g, role],
            device_id=(1 - k, row, col), device_id_type=MESH,
        )

    def to_z(g):
        mine = a_all.at[col, k]
        return pltpu.make_async_remote_copy(
            src_ref=mine, dst_ref=mine, send_sem=zsend.at[g - 1], recv_sem=zrecv.at[g - 1],
            device_id=(k, row, col ^ (4 * g)), device_id_type=MESH,
        )

    def to_y(g, what):
        zg = zl ^ g
        if what < 2:
            src = a_all.at[zg * 4 + y, k]
        elif what == 2:
            src = a_all.at[zg * 4 + ym, k, pl.ds(0, HALF)]
        else:
            src = a_all.at[zg * 4 + yp, k, pl.ds(HALF, HALF)]
        target = yp if what in (0, 2) else ym
        return pltpu.make_async_remote_copy(
            src_ref=src, dst_ref=src, send_sem=ysend.at[g, what], recv_sem=yrecv.at[g, what],
            device_id=(k, row, zl * 4 + target), device_id_type=MESH,
        )

    def arrived(piece, sem):
        pltpu.make_async_copy(piece, piece, sem).wait()

    def stage_a(g):
        if g:
            arrived(a_piece(g, 0, k), zrecv.at[g - 1])
        to_y(g, 0).start()
        to_y(g, 1).start()
        to_core(g, 0).start()

    def stage_b(g):
        arrived(a_piece(g, 1, k), yrecv.at[g, 0])
        to_y(g, 2).start()
        to_core(g, 1).start()
        arrived(a_piece(g, 2, k), yrecv.at[g, 1])
        to_y(g, 3).start()
        to_core(g, 2).start()

    def stage_c(g):
        arrived(a_piece(g, 3, k), yrecv.at[g, 2])
        to_core(g, 3).start()
        arrived(a_piece(g, 4, k), yrecv.at[g, 3])
        to_core(g, 4).start()

    for c in far:
        c.start()
    b_spread(0, 0)
    b_spread(0, 1)
    stage_a(0)
    for g in (1, 2, 3):
        to_z(g).start()

    loads[4].wait()
    f_tmp[0:1024, :] = w_in[...].astype(F32)
    for e in range(CHAN):
        e8, r = e // 4, e % 4
        part = f_tmp[pl.ds(e, CHAN, stride=CHAN), :].astype(BF16)
        for d in range(4):
            w_rot[d, pl.ds((e8 * 4 + (r + d) % 4) * CHAN, CHAN), :] = part

    jc = pl.multiple_of(j_first + k * NJ - j_win, 16)
    counts = lax.dot_general(
        jnp.concatenate([mt_j[s, pl.ds(jc, NJ), :] for s in range(2)], axis=1).astype(BF16),
        jnp.concatenate([mt_i[s] for s in range(2)], axis=1).astype(BF16),
        (((1,), (1,)), ((), ())),
        preferred_element_type=F32,
    )
    counts = jnp.where(i_first == i_win, counts[:, 0:192], counts[:, 64:256])
    recip = 1.0 / jnp.maximum(counts, 1.0)
    for z in range(4):
        rcs[z, :, 0:SLAB] = recip[:, z * SLAB:(z + 1) * SLAB]

    stage_b(0)
    stage_a(1)
    far[0].wait_recv()
    b_spread(1, 0)
    stage_b(1)
    far[1].wait_recv()
    b_spread(1, 1)
    stage_c(0)
    stage_a(2)
    stage_c(1)

    for slot in range(4):
        for s in range(2):
            for h in range(2):
                arrived(b_all.at[slot, s, pl.ds(h * HALF, HALF)], brecv.at[slot, s, h])
    for s in range(2):
        for slot in range(4):
            f_tmp[pl.ds(slot * ROWS, ROWS), :] = b_all[slot, s].astype(F32)
        for e in range(CHAN):
            e8, r = e // 4, e % 4
            part = f_tmp[pl.ds(e, NJ, stride=CHAN), :].astype(BF16)
            b_rot[r, pl.ds(e8 * NJ, NJ), pl.ds(s * LANES, LANES)] = part

    lane = lax.broadcasted_iota(jnp.int32, (NJ, 128), 1) // CHAN
    odd = (lane % 2) == 1
    high = lane >= 2
    bias = bias_ref[...]

    def slab(q, _):
        zg = zl ^ q
        for role in range(5):
            yy = (y, ym, yp, (y + 2) % 4, (y + 2) % 4)[role]
            first, size = PIECES[role]
            arrived(a_all.at[zg * 4 + yy, 1 - k, pl.ds(first, size)], crecv.at[q, role])

        for t in range(6):
            if t == 0:
                pl.when(q == 0)(lambda: stage_b(2))
            if t == 1:
                pl.when(q == 0)(lambda: stage_a(3))
            if t == 3:
                pl.when(q == 0)(lambda: stage_c(2))
            if t == 4:
                pl.when(q == 0)(lambda: stage_b(3))
            groups = []
            for h in range(2):
                chip, part = (t * 2 + h) // 3, (t * 2 + h) % 3
                groups.append([
                    jnp.concatenate(
                        [a_all[zg * 4 + chip, s, pl.ds(part * 128 + d * CHAN, CHAN), :] for s in range(2)], axis=1
                    )
                    for d in range(4)
                ])
            outer = []
            for r in range(4):
                rot = jnp.concatenate([grp[(g - r) % 4] for grp in groups for g in range(4)], axis=0)
                outer.append(
                    lax.dot_general(b_rot[r], rot, (((1,), (1,)), ((), ())), preferred_element_type=F32)
                )
            for h in range(2):
                rows = pl.ds((t * 2 + h) * NJ, NJ)
                for e8 in range(8):
                    v = [outer[r][e8 * NJ:(e8 + 1) * NJ, h * 128:(h + 1) * 128] for r in range(4)]
                    for d in range(4):
                        low = jnp.where(odd, v[(1 - d) % 4], v[(0 - d) % 4])
                        top = jnp.where(odd, v[(3 - d) % 4], v[(2 - d) % 4])
                        pairs[d, rows, pl.ds(e8 * 128, 128)] = jnp.where(high, top, low).astype(BF16)
        pl.when(q == 0)(lambda: stage_c(3))
        rc = rcs[zg]
        for d in range(4):
            acc = jnp.dot(pairs[d], w_rot[d], preferred_element_type=F32) + bias
            for grp in range(12):
                i = grp * 4 + d
                o_buf[zg * SLAB + i] = (acc[grp * NJ:(grp + 1) * NJ] * rc[:, i:i + 1]).astype(BF16)
        rows = pl.ds(zg * SLAB, SLAB)
        pltpu.make_async_copy(o_buf.at[rows], o_hbm.at[rows], out_sem.at[q]).start()
        return 0

    lax.fori_loop(0, 4, slab, 0)

    for c in far:
        c.wait_send()
    b_drain()
    for g in range(4):
        if g:
            to_z(g).wait_send()
        for what in range(4):
            to_y(g, what).wait_send()
        for role in range(5):
            to_core(g, role).wait_send()
    for q in range(4):
        rows = pl.ds((zl ^ q) * SLAB, SLAB)
        pltpu.make_async_copy(o_buf.at[rows], o_hbm.at[rows], out_sem.at[q]).wait()


def local(first, second, coverage, matrix, offset):
    seqs, block, chans = first.shape
    a = jnp.transpose(first, (1, 2, 0)).reshape(block * chans, seqs)
    b = jnp.transpose(second, (1, 2, 0)).reshape(block * chans, seqs)
    hbm = pl.BlockSpec(memory_space=pl.ANY)
    vmem = pl.BlockSpec(memory_space=pltpu.VMEM)
    dma = pltpu.SemaphoreType.DMA
    return pl.pallas_call(
        kernel,
        out_shape=jax.ShapeDtypeStruct((192, NJ, CZ), BF16),
        in_specs=[hbm, hbm, hbm, hbm, vmem],
        out_specs=hbm,
        scratch_shapes=[
            pltpu.VMEM((16, 2, ROWS, LANES), BF16),
            pltpu.VMEM((4, 2, ROWS, LANES), BF16),
            pltpu.VMEM((ROWS, LANES), BF16),
            pltpu.VMEM((ROWS, LANES), BF16),
            pltpu.VMEM((ROWS, LANES), BF16),
            pltpu.VMEM((256, 256), jnp.int32),
            pltpu.VMEM((256, 256), jnp.int32),
            pltpu.VMEM((2, 256, LANES), F32),
            pltpu.VMEM((2, 256, LANES), F32),
            pltpu.VMEM((1024, CZ), BF16),
            pltpu.VMEM((1536, 128), F32),
            pltpu.VMEM((4, 8 * NJ, 256), BF16),
            pltpu.VMEM((4, 1024, CZ), BF16),
            pltpu.VMEM((4, 12 * NJ, 1024), BF16),
            pltpu.VMEM((4, NJ, 128), F32),
            pltpu.VMEM((192, NJ, CZ), BF16),
            dma((5,)),
            dma((4,)),
            dma((2, 2, 4)),
            dma((4, 2, 2)),
            dma((2,)),
            dma((2,)),
            dma((3,)),
            dma((3,)),
            dma((4, 4)),
            dma((4, 4)),
            dma((4, 5)),
            dma((4, 5)),
        ],
        compiler_params=pltpu.CompilerParams(
            collective_id=0, has_side_effects=True, vmem_limit_bytes=56 * 2**20
        ),
        cost_estimate=pl.CostEstimate(flops=7 * 10**9, bytes_accessed=5 * 10**6, transcendentals=0),
    )(a, b, coverage, matrix, offset.reshape(1, CZ))


def solution(mesh):
    in_specs = (P("seq", ("row", "col"), None), P("seq", ("col", "row"), None), P(), P(), P())
    out_specs = P("row", ("col", "seq"), None)
    return jax.shard_map(local, mesh=mesh, in_specs=in_specs, out_specs=out_specs, check_vma=False)
```

```python
import jax
import jax.numpy as jnp
from jax import lax
from jax.experimental import pallas as pl
from jax.experimental.pallas import tpu as pltpu
from jax.sharding import PartitionSpec as P

MESH = pl.DeviceIdType.MESH
F32 = jnp.float32
BF16 = jnp.bfloat16

CHAN = 32
BLK = 12
ROWS = BLK * CHAN
PART = 4 * CHAN
HALF = PART // 2
LANES = 128
NJ = 48
CZ = 128
SPAN = 64
STRIDE = 56


def kernel(
    a_hbm, b_hbm, m_hbm, w_hbm, bias_hbm, o_ref,
    a_all, b_all, a_own, b_own, b_far, m_i, m_j, mt_i, mt_j, mt_a, w_in, bias_in, w_even_odd, perm, a_perm, b_split,
    outer, recip_tmp, recips, staged,
    load_sem, bsend, brecv, fsend, frecv, zsend, zrecv, ysend, yrecv, csend, crecv,
):
    k = lax.axis_index("seq")
    row = lax.axis_index("row")
    col = lax.axis_index("col")
    x, zh = row // 2, row % 2
    zl, y = col // 4, col % 4
    half = x // 2
    yp, ym = (y + 1) % 4, (y + 3) % 4

    i_first = row * 192
    j_first = col * 96
    i_win = pl.multiple_of((i_first // 128) * 128, 128)
    j_win = pl.multiple_of(jnp.minimum((j_first // 128) * 128, 1280), 128)
    loads = [
        pltpu.make_async_copy(m_hbm.at[:, pl.ds(i_win, 256)], m_i, load_sem.at[0]),
        pltpu.make_async_copy(m_hbm.at[:, pl.ds(j_win, 256)], m_j, load_sem.at[1]),
        pltpu.make_async_copy(a_hbm, a_own, load_sem.at[2]),
        pltpu.make_async_copy(b_hbm, b_own, load_sem.at[3]),
        pltpu.make_async_copy(w_hbm, w_in, load_sem.at[4]),
        pltpu.make_async_copy(bias_hbm, bias_in, load_sem.at[5]),
    ]
    for c in loads:
        c.start()

    barrier = pltpu.get_barrier_semaphore()
    peers = [(1 - k, row, col), (k, row ^ 1, col)]
    for dx in (1, 2, 3):
        peers += [(s, row ^ (2 * dx), col) for s in (0, 1)]
    peers += [(k, row, col ^ (4 * g)) for g in (1, 2, 3)]
    peers += [(k, row, zl * 4 + (y + dy) % 4) for dy in (1, 2, 3)]
    for p in peers:
        pl.semaphore_signal(barrier, inc=1, device_id=p, device_id_type=MESH)

    loads[0].wait()
    for s in range(2):
        mt_i[s] = m_i[pl.ds(s * LANES, LANES), :].astype(F32).T
    loads[1].wait()
    for s in range(2):
        mt_j[s] = m_j[pl.ds(s * LANES, LANES), :].astype(F32).T
    loads[3].wait()
    jo = j_first + row * BLK - j_win
    for n in range(BLK):
        flags = mt_j[k, pl.ds(jo + n, 1), :].astype(BF16)
        sl = pl.ds(n * CHAN, CHAN)
        b_own[sl, :] = b_own[sl, :] * flags
    loads[2].wait()
    i_off = pl.multiple_of(i_first - i_win, 64)
    for n in range(BLK):
        flags = mt_i[k, pl.ds(i_off + col * BLK + n, 1), :].astype(BF16)
        a_all[n // 4, k, 0, 0, pl.ds((n % 4) * CHAN, CHAN), :] = a_own[pl.ds(n * CHAN, CHAN), :] * flags

    pl.semaphore_wait(barrier, len(peers))

    far = [
        pltpu.make_async_remote_copy(
            src_ref=b_own.at[pl.ds(h * PART, PART)],
            dst_ref=b_far.at[pl.ds(h * PART, PART)],
            send_sem=fsend.at[h],
            recv_sem=frecv.at[h],
            device_id=(k, row ^ 1, col),
            device_id_type=MESH,
        )
        for h in range(3)
    ]

    def b_copy(h):
        rows = pl.ds(0, ROWS) if h is None else pl.ds(h * PART, PART)
        src = (b_own if h is None else b_far).at[rows]
        slot = (x % 2) * 2 + (zh if h is None else 1 - zh)
        dst = b_all.at[slot, k, rows]
        return src, dst, brecv.at[slot, k, h or 0], 3 if h is None else h

    def b_spread(h):
        src, dst, sem, n = b_copy(h)
        for dx in (2, 1, 3):
            pltpu.make_async_remote_copy(
                src_ref=src, dst_ref=dst, send_sem=bsend.at[n, dx], recv_sem=sem,
                device_id=(half, row ^ (2 * dx), col), device_id_type=MESH,
            ).start()

        @pl.when(half == k)
        def _():
            pltpu.make_async_copy(src, dst, sem).start()

        @pl.when(half != k)
        def _():
            pltpu.make_async_remote_copy(
                src_ref=src, dst_ref=dst, send_sem=bsend.at[n, 0], recv_sem=sem,
                device_id=(1 - k, row, col), device_id_type=MESH,
            ).start()

    def b_drain():
        for h in (None, 0, 1, 2):
            src, dst, sem, n = b_copy(h)
            for dx in range(4):

                def done():
                    pltpu.make_async_copy(src, src, bsend.at[n, dx]).wait()

                if dx:
                    done()
                else:
                    pl.when(half != k)(done)


    def remote(src, dst, send_sem, recv_sem, device):
        return pltpu.make_async_remote_copy(
            src_ref=src, dst_ref=dst, send_sem=send_sem, recv_sem=recv_sem, device_id=device, device_id_type=MESH
        )

    def to_core(r):
        piece = a_all.at[r, k]
        return remote(piece, piece, csend.at[r], crecv.at[r], (1 - k, row, col))

    def to_z(r, g):
        return remote(
            a_all.at[r, k, 0, 0], a_all.at[r, k, 0, g], zsend.at[r, g - 1], zrecv.at[r, g - 1], (k, row, col ^ (4 * g))
        )

    def to_y(r, rest, dy):
        sl = pl.ds(1, 3) if rest else pl.ds(0, 1)
        src, dst = a_all.at[r, k, 0, sl], a_all.at[r, k, dy, sl]
        target = zl * 4 + (yp, ym, (y + 2) % 4)[dy - 1]
        return remote(src, dst, ysend.at[r, rest, dy - 1], yrecv.at[r, rest, dy - 1], (k, row, target))

    def arrived(piece, sem):
        pltpu.make_async_copy(piece, piece, sem).wait()

    def z_send(r):
        to_z(r, 1).start()
        to_z(r, 2).start()

        to_z(r, 3).start()

    def stage_a(r):
        for g in (1, 2, 3):
            arrived(a_all.at[r, k, 0, g], zrecv.at[r, g - 1])
        for dy in (3, 1, 2):
            to_y(r, 1, dy).start()

    def stage_b(r):
        for dy in (1, 2, 3):
            arrived(a_all.at[r, k, dy, pl.ds(0, 1)], yrecv.at[r, 0, dy - 1])
            arrived(a_all.at[r, k, dy, pl.ds(1, 3)], yrecv.at[r, 1, dy - 1])
        to_core(r).start()

    def gathered(r):
        arrived(a_all.at[r, 1 - k], crecv.at[r])

    origin_col = [(zl ^ g) * 4 + yy for yy in (y, ym, yp, (y + 2) % 4) for g in range(4)]

    z_send(0)
    for c in far:
        c.start()
    for r in range(3):
        for dy in (3, 1, 2):
            to_y(r, 0, dy).start()
    b_spread(None)
    z_send(1)
    z_send(2)

    loads[4].wait()
    loads[5].wait()
    for odd in range(2):
        part = jnp.concatenate([w_in[pl.ds((2 * c + odd) * CHAN, CHAN), :] for c in range(16)], axis=0)
        w_even_odd[odd] = part.astype(F32).T.astype(BF16)
    bias = jnp.broadcast_to(bias_in[...], (CZ, CZ)).T
    out_row = lax.broadcasted_iota(jnp.int32, (256, 256), 0)
    in_row = lax.broadcasted_iota(jnp.int32, (256, 256), 1)
    perm[...] = (in_row == (out_row % 8) * CHAN + out_row // 8).astype(F32).astype(BF16)

    jc = pl.multiple_of(j_first + k * NJ - j_win, 16)
    flags_j = jnp.concatenate([mt_j[s, pl.ds(jc, NJ), :] for s in range(2)], axis=1).astype(BF16)
    for r in range(3):
        for s in range(2):
            for c in range(16):
                for n in range(4):
                    mt_a[s, pl.ds(c * 4 + n, 1), :] = mt_i[s, pl.ds(i_off + origin_col[c] * BLK + r * 4 + n, 1), :]
        flags_i = jnp.concatenate([mt_a[s] for s in range(2)], axis=1).astype(BF16)
        counts = lax.dot_general(flags_j, flags_i, (((1,), (1,)), ((), ())), preferred_element_type=F32)
        recip_tmp[:, 0:SPAN] = 1.0 / jnp.maximum(counts, 1.0)
        for odd in range(2):
            recips[r, :, pl.ds(odd * SPAN, SPAN)] = recip_tmp[pl.ds(odd, NJ // 2, stride=2), :][:, 0:SPAN]

    stage_a(0)
    stage_a(1)
    stage_a(2)
    for h in range(3):
        far[h].wait_recv()
        b_spread(h)
    stage_b(0)
    stage_b(1)

    def prepare_b():
        for xx in range(2):
            for s in range(2):
                arrived(b_all.at[xx * 2 + zh, s], brecv.at[xx * 2 + zh, s, 0])
        for h in range(3):
            for xx in range(2):
                for s in range(2):
                    slot = xx * 2 + 1 - zh
                    arrived(b_all.at[slot, s, pl.ds(h * PART, PART)], brecv.at[slot, s, h])
        for slot in range(4):
            for s in range(2):
                for n in range(BLK):
                    rows = pl.ds((slot * 6 + n // 2) * CHAN, CHAN)
                    b_split[n % 2, rows, pl.ds(s * LANES, LANES)] = b_all[slot, s, pl.ds(n * CHAN, CHAN), :]

    def prepare_a(r):
        for pair in range(4):
            moved = []
            for g in (2 * pair, 2 * pair + 1):
                block = jnp.concatenate(
                    [jnp.concatenate([a_all[r, s, g // 2, (2 * g + u) % 4] for s in range(2)], axis=1) for u in range(2)], axis=0
                )
                moved.append(jnp.dot(perm[...], block, preferred_element_type=F32))
            for c in range(CHAN):
                part = jnp.concatenate([v[c * 8:(c + 1) * 8] for v in moved], axis=0)
                a_perm[c, pl.ds(pair * 16, 16), :] = part.astype(BF16)

    def outer_step(ct):
        for odd in range(2):
            rows = []
            for c in (4 * ct, 4 * ct + 2):
                pair = [a_perm[c], a_perm[c + 1]]
                rows += pair[::-1] if odd else pair
            value = lax.dot_general(
                b_split[odd], jnp.concatenate(rows, axis=0), (((1,), (1,)), ((), ())), preferred_element_type=F32
            )
            outer[odd, :, pl.ds(ct * 256, 256)] = value.astype(BF16)

    def project_step(r, jp):
        low = lax.broadcasted_iota(jnp.int16, (CHAN, 128), 1) < SPAN
        left, right = [], []
        for u in range(2):
            rows = pl.ds((jp + u) * CHAN, CHAN)
            keep, swap = [], []
            for c in range(16):
                v0 = outer[0, rows, pl.ds(c * 128, 128)]
                v1 = outer[1, rows, pl.ds(c * 128, 128)]
                keep.append(jnp.where(low, v0, v1))
                swap.append(jnp.where(low, v1, v0))
            left.append(jnp.concatenate(keep, axis=0))
            right.append(jnp.concatenate(swap, axis=0))
        acc0 = jnp.dot(w_even_odd[0], jnp.concatenate(left, axis=1), preferred_element_type=F32)
        acc1 = jnp.dot(w_even_odd[1], jnp.concatenate(right, axis=1), preferred_element_type=F32)
        for u in range(2):
            lanes = slice(u * 128, (u + 1) * 128)
            value = acc0[:, lanes] + pltpu.roll(acc1[:, lanes], SPAN, 1) + bias
            value = (value * recips[r, pl.ds(jp + u, 1), :]).T
            j = 2 * (jp + u)
            staged[pl.ds(j, SPAN, stride=STRIDE), :] = value[0:SPAN]
            staged[pl.ds(j + 1, SPAN, stride=STRIDE), :] = value[SPAN:2 * SPAN]

    def finish(r):
        for c in range(16):
            for n in range(4):
                i = c * 4 + n
                o_ref[origin_col[c] * BLK + r * 4 + n] = staged[pl.ds(i * STRIDE, NJ), :].astype(BF16)

    events = {(0, 10): lambda: stage_b(2)}
    prepare_b()
    for r in range(3):
        gathered(r)
        prepare_a(r)
        for n in range(20):
            if n < 8:
                outer_step(n)
            else:
                project_step(r, 2 * (n - 8))
            if (r, n) in events:
                events[r, n]()
        finish(r)

    for c in far:
        c.wait_send()
    b_drain()
    for r in range(3):
        to_z(r, 1).wait_send()
        to_z(r, 2).wait_send()

        to_z(r, 3).wait_send()

        for rest in range(2):
            for dy in (1, 2, 3):
                to_y(r, rest, dy).wait_send()
        to_core(r).wait_send()


def local(first, second, coverage, matrix, offset):
    seqs, block, chans = first.shape
    a = jnp.transpose(first, (1, 2, 0)).reshape(block * chans, seqs)
    b = jnp.transpose(second, (1, 2, 0)).reshape(block * chans, seqs)
    hbm = pl.BlockSpec(memory_space=pltpu.HBM)
    dma = pltpu.SemaphoreType.DMA
    return pl.pallas_call(
        kernel,
        out_shape=pltpu.VMEM((192, NJ, CZ), BF16),
        in_specs=[hbm] * 5,
        out_specs=pl.BlockSpec(memory_space=pltpu.VMEM),
        scratch_shapes=[
            pltpu.VMEM((3, 2, 4, 4, PART, LANES), BF16),
            pltpu.VMEM((4, 2, ROWS, LANES), BF16),
            pltpu.VMEM((ROWS, LANES), BF16),
            pltpu.VMEM((ROWS, LANES), BF16),
            pltpu.VMEM((ROWS, LANES), BF16),
            pltpu.VMEM((256, 256), jnp.int32),
            pltpu.VMEM((256, 256), jnp.int32),
            pltpu.VMEM((2, 256, LANES), F32),
            pltpu.VMEM((2, 256, LANES), F32),
            pltpu.VMEM((2, SPAN, LANES), F32),
            pltpu.VMEM((1024, CZ), BF16),
            pltpu.VMEM((1, CZ), F32),
            pltpu.VMEM((2, CZ, 512), BF16),
            pltpu.VMEM((256, 256), BF16),
            pltpu.VMEM((CHAN, SPAN, 256), BF16),
            pltpu.VMEM((2, 768, 256), BF16),
            pltpu.VMEM((2, 768, 2048), BF16),
            pltpu.VMEM((NJ, 128), F32),
            pltpu.VMEM((3, NJ // 2, 128), F32),
            pltpu.VMEM((SPAN * STRIDE, CZ), F32),
            dma((6,)),
            dma((4, 4)),
            dma((4, 2, 3)),
            dma((3,)),
            dma((3,)),
            dma((3, 3)),
            dma((3, 3)),
            dma((3, 2, 3)),
            dma((3, 2, 3)),
            dma((3,)),
            dma((3,)),
        ],
        compiler_params=pltpu.CompilerParams(
            collective_id=0, has_side_effects=True, vmem_limit_bytes=52 * 2**20
        ),
        cost_estimate=pl.CostEstimate(flops=7 * 10**9, bytes_accessed=5 * 10**6, transcendentals=0),
    )(a, b, coverage, matrix, offset.reshape(1, CZ))


def solution(mesh):
    in_specs = (P("seq", ("row", "col"), None), P("seq", ("col", "row"), None), P(), P(), P())
    out_specs = P("row", ("col", "seq"), None)
    return jax.shard_map(local, mesh=mesh, in_specs=in_specs, out_specs=out_specs, check_vma=False)
```

```python
import jax
import jax.numpy as jnp
from jax import lax
from jax.experimental import pallas as pl
from jax.experimental.pallas import tpu as pltpu
from jax.sharding import PartitionSpec as P

MESH = pl.DeviceIdType.MESH
F32 = jnp.float32
BF16 = jnp.bfloat16

CHAN = 32
BLK = 12
ROWS = BLK * CHAN
PART = 4 * CHAN
LANES = 128
NJ = 48
CZ = 128
SPAN = 64
STRIDE = 56


def kernel(
    a_hbm, b_hbm, m_hbm, w_hbm, bias_hbm, o_ref,
    a_all, b_all, a_own, b_own, b_far, m_i, m_j, mt_i, mt_j, mt_a, w_in, bias_in, w_even_odd, perm, a_perm, b_split,
    outer, recip_tmp, recips, staged,
    load_sem, bsend, brecv, fsend, frecv, zsend, zrecv, ysend, yrecv, csend, crecv,
):
    k = lax.axis_index("seq")
    row = lax.axis_index("row")
    col = lax.axis_index("col")
    x, zh = row // 2, row % 2
    zl, y = col // 4, col % 4
    half = x // 2
    yp, ym = (y + 1) % 4, (y + 3) % 4

    i_first = row * 192
    j_first = col * 96
    i_win = pl.multiple_of((i_first // 128) * 128, 128)
    j_win = pl.multiple_of(jnp.minimum((j_first // 128) * 128, 1280), 128)
    loads = [
        pltpu.make_async_copy(m_hbm.at[:, pl.ds(i_win, 256)], m_i, load_sem.at[0]),
        pltpu.make_async_copy(m_hbm.at[:, pl.ds(j_win, 256)], m_j, load_sem.at[1]),
        pltpu.make_async_copy(a_hbm, a_own, load_sem.at[2]),
        pltpu.make_async_copy(b_hbm, b_own, load_sem.at[3]),
        pltpu.make_async_copy(w_hbm, w_in, load_sem.at[4]),
        pltpu.make_async_copy(bias_hbm, bias_in, load_sem.at[5]),
    ]
    for c in loads:
        c.start()

    barrier = pltpu.get_barrier_semaphore()
    peers = [(1 - k, row, col), (k, row ^ 1, col)]
    for dx in (1, 2, 3):
        peers += [(s, row ^ (2 * dx), col) for s in (0, 1)]
    peers += [(k, row, col ^ (4 * g)) for g in (1, 2, 3)]
    peers += [(k, row, zl * 4 + (y + dy) % 4) for dy in (1, 2, 3)]
    for p in peers:
        pl.semaphore_signal(barrier, inc=1, device_id=p, device_id_type=MESH)

    loads[0].wait()
    for s in range(2):
        mt_i[s] = m_i[pl.ds(s * LANES, LANES), :].astype(F32).T
    loads[1].wait()
    for s in range(2):
        mt_j[s] = m_j[pl.ds(s * LANES, LANES), :].astype(F32).T
    loads[3].wait()
    jo = j_first + row * BLK - j_win
    for n in range(BLK):
        flags = mt_j[k, pl.ds(jo + n, 1), :].astype(BF16)
        sl = pl.ds(n * CHAN, CHAN)
        b_own[sl, :] = b_own[sl, :] * flags
    loads[2].wait()
    i_off = pl.multiple_of(i_first - i_win, 64)
    for n in range(BLK):
        flags = mt_i[k, pl.ds(i_off + col * BLK + n, 1), :].astype(BF16)
        a_all[n // 4, k, 0, 0, pl.ds((n % 4) * CHAN, CHAN), :] = a_own[pl.ds(n * CHAN, CHAN), :] * flags

    pl.semaphore_wait(barrier, len(peers))

    far = [
        pltpu.make_async_remote_copy(
            src_ref=b_own.at[pl.ds(h * PART, PART)],
            dst_ref=b_far.at[pl.ds(h * PART, PART)],
            send_sem=fsend.at[h],
            recv_sem=frecv.at[h],
            device_id=(k, row ^ 1, col),
            device_id_type=MESH,
        )
        for h in range(3)
    ]

    def b_copy(h):
        rows = pl.ds(0, ROWS) if h is None else pl.ds(h * PART, PART)
        src = (b_own if h is None else b_far).at[rows]
        slot = (x % 2) * 2 + (zh if h is None else 1 - zh)
        dst = b_all.at[slot, k, rows]
        return src, dst, brecv.at[slot, k, h or 0], 3 if h is None else h

    def b_spread(h):
        src, dst, sem, n = b_copy(h)
        for dx in (2, 1, 3):
            pltpu.make_async_remote_copy(
                src_ref=src, dst_ref=dst, send_sem=bsend.at[n, dx], recv_sem=sem,
                device_id=(half, row ^ (2 * dx), col), device_id_type=MESH,
            ).start()

        @pl.when(half == k)
        def _():
            pltpu.make_async_copy(src, dst, sem).start()

        @pl.when(half != k)
        def _():
            pltpu.make_async_remote_copy(
                src_ref=src, dst_ref=dst, send_sem=bsend.at[n, 0], recv_sem=sem,
                device_id=(1 - k, row, col), device_id_type=MESH,
            ).start()

    def b_drain():
        for h in (None, 0, 1, 2):
            src, dst, sem, n = b_copy(h)
            for dx in range(4):

                def done():
                    pltpu.make_async_copy(src, src, bsend.at[n, dx]).wait()

                if dx:
                    done()
                else:
                    pl.when(half != k)(done)


    def remote(src, dst, send_sem, recv_sem, device):
        return pltpu.make_async_remote_copy(
            src_ref=src, dst_ref=dst, send_sem=send_sem, recv_sem=recv_sem, device_id=device, device_id_type=MESH
        )

    def to_core(r, dy):
        piece = a_all.at[r, k, dy]
        return remote(piece, piece, csend.at[r, dy], crecv.at[r, dy], (1 - k, row, col))

    def to_z(r, g):
        return remote(
            a_all.at[r, k, 0, 0], a_all.at[r, k, 0, g], zsend.at[r, g - 1], zrecv.at[r, g - 1], (k, row, col ^ (4 * g))
        )

    def to_y(r, rest, dy):
        sl = pl.ds(1, 3) if rest else pl.ds(0, 1)
        src, dst = a_all.at[r, k, 0, sl], a_all.at[r, k, dy, sl]
        target = zl * 4 + (yp, ym, (y + 2) % 4)[dy - 1]
        return remote(src, dst, ysend.at[r, rest, dy - 1], yrecv.at[r, rest, dy - 1], (k, row, target))

    def arrived(piece, sem):
        pltpu.make_async_copy(piece, piece, sem).wait()

    def z_send(r):
        to_z(r, 1).start()
        to_z(r, 2).start()

        to_z(r, 3).start()

    def stage_a(r):
        for g in (1, 2, 3):
            arrived(a_all.at[r, k, 0, g], zrecv.at[r, g - 1])
        for dy in (3, 1, 2):
            to_y(r, 1, dy).start()
        to_core(r, 0).start()

    def stage_b(r):
        for dy in (1, 2, 3):
            arrived(a_all.at[r, k, dy, pl.ds(0, 1)], yrecv.at[r, 0, dy - 1])
            arrived(a_all.at[r, k, dy, pl.ds(1, 3)], yrecv.at[r, 1, dy - 1])
            to_core(r, dy).start()

    def gathered(r):
        for dy in range(4):
            arrived(a_all.at[r, 1 - k, dy], crecv.at[r, dy])

    origin_col = [(zl ^ g) * 4 + yy for yy in (y, ym, yp, (y + 2) % 4) for g in range(4)]

    z_send(0)
    for c in far:
        c.start()
    for r in range(3):
        for dy in (3, 1, 2):
            to_y(r, 0, dy).start()
    b_spread(None)

    loads[4].wait()
    loads[5].wait()
    for odd in range(2):
        part = jnp.concatenate([w_in[pl.ds((2 * c + odd) * CHAN, CHAN), :] for c in range(16)], axis=0)
        w_even_odd[odd] = part.astype(F32).T.astype(BF16)
    bias = jnp.broadcast_to(bias_in[...], (CZ, CZ)).T
    out_row = lax.broadcasted_iota(jnp.int32, (256, 256), 0)
    in_row = lax.broadcasted_iota(jnp.int32, (256, 256), 1)
    perm[...] = (in_row == (out_row % 8) * CHAN + out_row // 8).astype(F32).astype(BF16)

    jc = pl.multiple_of(j_first + k * NJ - j_win, 16)
    flags_j = jnp.concatenate([mt_j[s, pl.ds(jc, NJ), :] for s in range(2)], axis=1).astype(BF16)
    for r in range(3):
        for s in range(2):
            for c in range(16):
                for n in range(4):
                    mt_a[s, pl.ds(c * 4 + n, 1), :] = mt_i[s, pl.ds(i_off + origin_col[c] * BLK + r * 4 + n, 1), :]
        flags_i = jnp.concatenate([mt_a[s] for s in range(2)], axis=1).astype(BF16)
        counts = lax.dot_general(flags_j, flags_i, (((1,), (1,)), ((), ())), preferred_element_type=F32)
        recip_tmp[:, 0:SPAN] = 1.0 / jnp.maximum(counts, 1.0)
        for odd in range(2):
            recips[r, :, pl.ds(odd * SPAN, SPAN)] = recip_tmp[pl.ds(odd, NJ // 2, stride=2), :][:, 0:SPAN]

    stage_a(0)
    z_send(1)
    for h in range(3):
        far[h].wait_recv()
        b_spread(h)
    z_send(2)
    stage_a(1)
    stage_b(0)
    stage_a(2)

    def prepare_b():
        for xx in range(2):
            for s in range(2):
                arrived(b_all.at[xx * 2 + zh, s], brecv.at[xx * 2 + zh, s, 0])
        for h in range(3):
            for xx in range(2):
                for s in range(2):
                    slot = xx * 2 + 1 - zh
                    arrived(b_all.at[slot, s, pl.ds(h * PART, PART)], brecv.at[slot, s, h])
        for slot in range(4):
            for s in range(2):
                for n in range(BLK):
                    rows = pl.ds((slot * 6 + n // 2) * CHAN, CHAN)
                    b_split[n % 2, rows, pl.ds(s * LANES, LANES)] = b_all[slot, s, pl.ds(n * CHAN, CHAN), :]

    def prepare_a(r):
        for pair in range(4):
            moved = []
            for g in (2 * pair, 2 * pair + 1):
                block = jnp.concatenate(
                    [jnp.concatenate([a_all[r, s, g // 2, (2 * g + u) % 4] for s in range(2)], axis=1) for u in range(2)], axis=0
                )
                moved.append(jnp.dot(perm[...], block, preferred_element_type=F32))
            for c in range(CHAN):
                part = jnp.concatenate([v[c * 8:(c + 1) * 8] for v in moved], axis=0)
                a_perm[c, pl.ds(pair * 16, 16), :] = part.astype(BF16)

    def outer_step(ct):
        for odd in range(2):
            rows = []
            for c in (4 * ct, 4 * ct + 2):
                pair = [a_perm[c], a_perm[c + 1]]
                rows += pair[::-1] if odd else pair
            value = lax.dot_general(
                b_split[odd], jnp.concatenate(rows, axis=0), (((1,), (1,)), ((), ())), preferred_element_type=F32
            )
            outer[odd, :, pl.ds(ct * 256, 256)] = value.astype(BF16)

    def project_step(r, jp):
        low = lax.broadcasted_iota(jnp.int16, (CHAN, 128), 1) < SPAN
        left, right = [], []
        for u in range(2):
            rows = pl.ds((jp + u) * CHAN, CHAN)
            keep, swap = [], []
            for c in range(16):
                v0 = outer[0, rows, pl.ds(c * 128, 128)]
                v1 = outer[1, rows, pl.ds(c * 128, 128)]
                keep.append(jnp.where(low, v0, v1))
                swap.append(jnp.where(low, v1, v0))
            left.append(jnp.concatenate(keep, axis=0))
            right.append(jnp.concatenate(swap, axis=0))
        acc0 = jnp.dot(w_even_odd[0], jnp.concatenate(left, axis=1), preferred_element_type=F32)
        acc1 = jnp.dot(w_even_odd[1], jnp.concatenate(right, axis=1), preferred_element_type=F32)
        for u in range(2):
            lanes = slice(u * 128, (u + 1) * 128)
            value = acc0[:, lanes] + pltpu.roll(acc1[:, lanes], SPAN, 1) + bias
            value = (value * recips[r, pl.ds(jp + u, 1), :]).T
            j = 2 * (jp + u)
            staged[pl.ds(j, SPAN, stride=STRIDE), :] = value[0:SPAN]
            staged[pl.ds(j + 1, SPAN, stride=STRIDE), :] = value[SPAN:2 * SPAN]

    def finish(r):
        for c in range(16):
            for n in range(4):
                i = c * 4 + n
                o_ref[origin_col[c] * BLK + r * 4 + n] = staged[pl.ds(i * STRIDE, NJ), :].astype(BF16)

    events = {(0, 12): lambda: stage_b(1), (1, 10): lambda: stage_b(2)}
    prepare_b()
    for r in range(3):
        gathered(r)
        prepare_a(r)
        for n in range(20):
            if n < 8:
                outer_step(n)
            else:
                project_step(r, 2 * (n - 8))
            if (r, n) in events:
                events[r, n]()
        finish(r)

    for c in far:
        c.wait_send()
    b_drain()
    for r in range(3):
        to_z(r, 1).wait_send()
        to_z(r, 2).wait_send()

        to_z(r, 3).wait_send()

        for dy in (1, 2, 3):
            for rest in range(2):
                to_y(r, rest, dy).wait_send()
        for dy in range(4):
            to_core(r, dy).wait_send()


def local(first, second, coverage, matrix, offset):
    seqs, block, chans = first.shape
    a = jnp.transpose(first, (1, 2, 0)).reshape(block * chans, seqs)
    b = jnp.transpose(second, (1, 2, 0)).reshape(block * chans, seqs)
    hbm = pl.BlockSpec(memory_space=pltpu.HBM)
    dma = pltpu.SemaphoreType.DMA
    return pl.pallas_call(
        kernel,
        out_shape=pltpu.VMEM((192, NJ, CZ), BF16),
        in_specs=[hbm] * 5,
        out_specs=pl.BlockSpec(memory_space=pltpu.VMEM),
        scratch_shapes=[
            pltpu.VMEM((3, 2, 4, 4, PART, LANES), BF16),
            pltpu.VMEM((4, 2, ROWS, LANES), BF16),
            pltpu.VMEM((ROWS, LANES), BF16),
            pltpu.VMEM((ROWS, LANES), BF16),
            pltpu.VMEM((ROWS, LANES), BF16),
            pltpu.VMEM((256, 256), jnp.int32),
            pltpu.VMEM((256, 256), jnp.int32),
            pltpu.VMEM((2, 256, LANES), F32),
            pltpu.VMEM((2, 256, LANES), F32),
            pltpu.VMEM((2, SPAN, LANES), F32),
            pltpu.VMEM((1024, CZ), BF16),
            pltpu.VMEM((1, CZ), F32),
            pltpu.VMEM((2, CZ, 512), BF16),
            pltpu.VMEM((256, 256), BF16),
            pltpu.VMEM((CHAN, SPAN, 256), BF16),
            pltpu.VMEM((2, 768, 256), BF16),
            pltpu.VMEM((2, 768, 2048), BF16),
            pltpu.VMEM((NJ, 128), F32),
            pltpu.VMEM((3, NJ // 2, 128), F32),
            pltpu.VMEM((SPAN * STRIDE, CZ), F32),
            dma((6,)),
            dma((4, 4)),
            dma((4, 2, 3)),
            dma((3,)),
            dma((3,)),
            dma((3, 3)),
            dma((3, 3)),
            dma((3, 2, 3)),
            dma((3, 2, 3)),
            dma((3, 4)),
            dma((3, 4)),
        ],
        compiler_params=pltpu.CompilerParams(
            collective_id=0, has_side_effects=True, vmem_limit_bytes=52 * 2**20
        ),
        cost_estimate=pl.CostEstimate(flops=7 * 10**9, bytes_accessed=5 * 10**6, transcendentals=0),
    )(a, b, coverage, matrix, offset.reshape(1, CZ))


def solution(mesh):
    in_specs = (P("seq", ("row", "col"), None), P("seq", ("col", "row"), None), P(), P(), P())
    out_specs = P("row", ("col", "seq"), None)
    return jax.shard_map(local, mesh=mesh, in_specs=in_specs, out_specs=out_specs, check_vma=False)
```

```python
import jax
import jax.numpy as jnp
from jax import lax
from jax.experimental import pallas as pl
from jax.experimental.pallas import tpu as pltpu
from jax.sharding import PartitionSpec as P

MESH = pl.DeviceIdType.MESH
F32 = jnp.float32
BF16 = jnp.bfloat16

CHAN = 32
BLK = 12
ROWS = BLK * CHAN
PART = 4 * CHAN
LANES = 128
NJ = 48
CZ = 128
SPAN = 64
STRIDE = 56


def kernel(
    a_hbm, b_hbm, m_hbm, w_hbm, bias_hbm, o_ref,
    a_all, b_all, a_own, b_own, b_far, m_i, m_j, mt_i, mt_j, mt_a, w_in, bias_in, w_even_odd, perm, a_perm, b_split,
    outer, recip_tmp, recips, staged,
    load_sem, bsend, brecv, fsend, frecv, zsend, zrecv, ysend, yrecv, csend, crecv,
):
    k = lax.axis_index("seq")
    row = lax.axis_index("row")
    col = lax.axis_index("col")
    x, zh = row // 2, row % 2
    zl, y = col // 4, col % 4
    half = x // 2
    yp, ym = (y + 1) % 4, (y + 3) % 4

    i_first = row * 192
    j_first = col * 96
    i_win = pl.multiple_of((i_first // 128) * 128, 128)
    j_win = pl.multiple_of(jnp.minimum((j_first // 128) * 128, 1280), 128)
    loads = [
        pltpu.make_async_copy(m_hbm.at[:, pl.ds(i_win, 256)], m_i, load_sem.at[0]),
        pltpu.make_async_copy(m_hbm.at[:, pl.ds(j_win, 256)], m_j, load_sem.at[1]),
        pltpu.make_async_copy(a_hbm, a_own, load_sem.at[2]),
        pltpu.make_async_copy(b_hbm, b_own, load_sem.at[3]),
        pltpu.make_async_copy(w_hbm, w_in, load_sem.at[4]),
        pltpu.make_async_copy(bias_hbm, bias_in, load_sem.at[5]),
    ]
    for c in loads:
        c.start()

    barrier = pltpu.get_barrier_semaphore()
    peers = [(1 - k, row, col), (k, row ^ 1, col)]
    for dx in (1, 2, 3):
        peers += [(s, row ^ (2 * dx), col) for s in (0, 1)]
    peers += [(k, row, col ^ (4 * g)) for g in (1, 2, 3)]
    peers += [(k, row, zl * 4 + (y + dy) % 4) for dy in (1, 2, 3)]
    for p in peers:
        pl.semaphore_signal(barrier, inc=1, device_id=p, device_id_type=MESH)

    loads[0].wait()
    for s in range(2):
        mt_i[s] = m_i[pl.ds(s * LANES, LANES), :].astype(F32).T
    loads[1].wait()
    for s in range(2):
        mt_j[s] = m_j[pl.ds(s * LANES, LANES), :].astype(F32).T
    loads[3].wait()
    jo = j_first + row * BLK - j_win
    for n in range(BLK):
        flags = mt_j[k, pl.ds(jo + n, 1), :].astype(BF16)
        sl = pl.ds(n * CHAN, CHAN)
        b_own[sl, :] = b_own[sl, :] * flags
    loads[2].wait()
    i_off = pl.multiple_of(i_first - i_win, 64)
    for n in range(BLK):
        flags = mt_i[k, pl.ds(i_off + col * BLK + n, 1), :].astype(BF16)
        a_all[n // 4, k, 0, 0, pl.ds((n % 4) * CHAN, CHAN), :] = a_own[pl.ds(n * CHAN, CHAN), :] * flags

    pl.semaphore_wait(barrier, len(peers))

    far = [
        pltpu.make_async_remote_copy(
            src_ref=b_own.at[pl.ds(h * PART, PART)],
            dst_ref=b_far.at[pl.ds(h * PART, PART)],
            send_sem=fsend.at[h],
            recv_sem=frecv.at[h],
            device_id=(k, row ^ 1, col),
            device_id_type=MESH,
        )
        for h in range(3)
    ]

    def b_copy(h):
        rows = pl.ds(0, ROWS) if h is None else pl.ds(h * PART, PART)
        src = (b_own if h is None else b_far).at[rows]
        slot = (x % 2) * 2 + (zh if h is None else 1 - zh)
        dst = b_all.at[slot, k, rows]
        return src, dst, brecv.at[slot, k, h or 0], 3 if h is None else h

    def b_spread(h):
        src, dst, sem, n = b_copy(h)
        for dx in (2, 1, 3):
            pltpu.make_async_remote_copy(
                src_ref=src, dst_ref=dst, send_sem=bsend.at[n, dx], recv_sem=sem,
                device_id=(half, row ^ (2 * dx), col), device_id_type=MESH,
            ).start()

        @pl.when(half == k)
        def _():
            pltpu.make_async_copy(src, dst, sem).start()

        @pl.when(half != k)
        def _():
            pltpu.make_async_remote_copy(
                src_ref=src, dst_ref=dst, send_sem=bsend.at[n, 0], recv_sem=sem,
                device_id=(1 - k, row, col), device_id_type=MESH,
            ).start()

    def b_drain():
        for h in (None, 0, 1, 2):
            src, dst, sem, n = b_copy(h)
            for dx in range(4):

                def done():
                    pltpu.make_async_copy(src, src, bsend.at[n, dx]).wait()

                if dx:
                    done()
                else:
                    pl.when(half != k)(done)


    def remote(src, dst, send_sem, recv_sem, device):
        return pltpu.make_async_remote_copy(
            src_ref=src, dst_ref=dst, send_sem=send_sem, recv_sem=recv_sem, device_id=device, device_id_type=MESH
        )

    def to_core(r, dy):
        piece = a_all.at[r, k, dy]
        return remote(piece, piece, csend.at[r, dy], crecv.at[r, dy], (1 - k, row, col))

    def to_z(r, g):
        return remote(
            a_all.at[r, k, 0, 0], a_all.at[r, k, 0, g], zsend.at[r, g - 1], zrecv.at[r, g - 1], (k, row, col ^ (4 * g))
        )

    def to_y(r, rest, dy):
        sl = pl.ds(1, 3) if rest else pl.ds(0, 1)
        src, dst = a_all.at[r, k, 0, sl], a_all.at[r, k, dy, sl]
        target = zl * 4 + (yp, ym, (y + 2) % 4)[dy - 1]
        return remote(src, dst, ysend.at[r, rest, dy - 1], yrecv.at[r, rest, dy - 1], (k, row, target))

    def arrived(piece, sem):
        pltpu.make_async_copy(piece, piece, sem).wait()

    def z_send(r):
        to_z(r, 1).start()
        to_z(r, 2).start()

        to_z(r, 3).start()

    def stage_a(r):
        for g in (1, 2, 3):
            arrived(a_all.at[r, k, 0, g], zrecv.at[r, g - 1])
        for dy in (1, 2, 3):
            to_y(r, 1, dy).start()
        to_core(r, 0).start()

    def stage_b(r):
        for dy in (1, 2, 3):
            arrived(a_all.at[r, k, dy, pl.ds(0, 1)], yrecv.at[r, 0, dy - 1])
            arrived(a_all.at[r, k, dy, pl.ds(1, 3)], yrecv.at[r, 1, dy - 1])
            to_core(r, dy).start()

    def gathered(r):
        for dy in range(4):
            arrived(a_all.at[r, 1 - k, dy], crecv.at[r, dy])

    origin_col = [(zl ^ g) * 4 + yy for yy in (y, ym, yp, (y + 2) % 4) for g in range(4)]

    z_send(0)
    for c in far:
        c.start()
    for r in range(3):
        for dy in (1, 2, 3):
            to_y(r, 0, dy).start()
    b_spread(None)

    loads[4].wait()
    loads[5].wait()
    for odd in range(2):
        part = jnp.concatenate([w_in[pl.ds((2 * c + odd) * CHAN, CHAN), :] for c in range(16)], axis=0)
        w_even_odd[odd] = part.astype(F32).T.astype(BF16)
    bias = jnp.broadcast_to(bias_in[...], (CZ, CZ)).T
    out_row = lax.broadcasted_iota(jnp.int32, (256, 256), 0)
    in_row = lax.broadcasted_iota(jnp.int32, (256, 256), 1)
    perm[...] = (in_row == (out_row % 8) * CHAN + out_row // 8).astype(F32).astype(BF16)

    jc = pl.multiple_of(j_first + k * NJ - j_win, 16)
    flags_j = jnp.concatenate([mt_j[s, pl.ds(jc, NJ), :] for s in range(2)], axis=1).astype(BF16)
    for r in range(3):
        for s in range(2):
            for c in range(16):
                for n in range(4):
                    mt_a[s, pl.ds(c * 4 + n, 1), :] = mt_i[s, pl.ds(i_off + origin_col[c] * BLK + r * 4 + n, 1), :]
        flags_i = jnp.concatenate([mt_a[s] for s in range(2)], axis=1).astype(BF16)
        counts = lax.dot_general(flags_j, flags_i, (((1,), (1,)), ((), ())), preferred_element_type=F32)
        recip_tmp[:, 0:SPAN] = 1.0 / jnp.maximum(counts, 1.0)
        for odd in range(2):
            recips[r, :, pl.ds(odd * SPAN, SPAN)] = recip_tmp[pl.ds(odd, NJ // 2, stride=2), :][:, 0:SPAN]

    stage_a(0)
    z_send(1)
    for h in range(3):
        far[h].wait_recv()
        b_spread(h)
    z_send(2)
    stage_a(1)
    stage_b(0)
    stage_a(2)

    def prepare_b():
        for xx in range(2):
            for s in range(2):
                arrived(b_all.at[xx * 2 + zh, s], brecv.at[xx * 2 + zh, s, 0])
        for h in range(3):
            for xx in range(2):
                for s in range(2):
                    slot = xx * 2 + 1 - zh
                    arrived(b_all.at[slot, s, pl.ds(h * PART, PART)], brecv.at[slot, s, h])
        for slot in range(4):
            for s in range(2):
                for n in range(BLK):
                    rows = pl.ds((slot * 6 + n // 2) * CHAN, CHAN)
                    b_split[n % 2, rows, pl.ds(s * LANES, LANES)] = b_all[slot, s, pl.ds(n * CHAN, CHAN), :]

    def prepare_a(r):
        for pair in range(4):
            moved = []
            for g in (2 * pair, 2 * pair + 1):
                block = jnp.concatenate(
                    [jnp.concatenate([a_all[r, s, g // 2, (2 * g + u) % 4] for s in range(2)], axis=1) for u in range(2)], axis=0
                )
                moved.append(jnp.dot(perm[...], block, preferred_element_type=F32))
            for c in range(CHAN):
                part = jnp.concatenate([v[c * 8:(c + 1) * 8] for v in moved], axis=0)
                a_perm[c, pl.ds(pair * 16, 16), :] = part.astype(BF16)

    def outer_step(ct):
        for odd in range(2):
            rows = []
            for c in (4 * ct, 4 * ct + 2):
                pair = [a_perm[c], a_perm[c + 1]]
                rows += pair[::-1] if odd else pair
            value = lax.dot_general(
                b_split[odd], jnp.concatenate(rows, axis=0), (((1,), (1,)), ((), ())), preferred_element_type=F32
            )
            outer[odd, :, pl.ds(ct * 256, 256)] = value.astype(BF16)

    def project_step(r, jp):
        low = lax.broadcasted_iota(jnp.int16, (CHAN, 128), 1) < SPAN
        left, right = [], []
        for u in range(2):
            rows = pl.ds((jp + u) * CHAN, CHAN)
            keep, swap = [], []
            for c in range(16):
                v0 = outer[0, rows, pl.ds(c * 128, 128)]
                v1 = outer[1, rows, pl.ds(c * 128, 128)]
                keep.append(jnp.where(low, v0, v1))
                swap.append(jnp.where(low, v1, v0))
            left.append(jnp.concatenate(keep, axis=0))
            right.append(jnp.concatenate(swap, axis=0))
        acc0 = jnp.dot(w_even_odd[0], jnp.concatenate(left, axis=1), preferred_element_type=F32)
        acc1 = jnp.dot(w_even_odd[1], jnp.concatenate(right, axis=1), preferred_element_type=F32)
        for u in range(2):
            lanes = slice(u * 128, (u + 1) * 128)
            value = acc0[:, lanes] + pltpu.roll(acc1[:, lanes], SPAN, 1) + bias
            value = (value * recips[r, pl.ds(jp + u, 1), :]).T
            j = 2 * (jp + u)
            staged[pl.ds(j, SPAN, stride=STRIDE), :] = value[0:SPAN]
            staged[pl.ds(j + 1, SPAN, stride=STRIDE), :] = value[SPAN:2 * SPAN]

    def finish(r):
        for c in range(16):
            for n in range(4):
                i = c * 4 + n
                o_ref[origin_col[c] * BLK + r * 4 + n] = staged[pl.ds(i * STRIDE, NJ), :].astype(BF16)

    events = {(0, 8): lambda: stage_b(1), (1, 1): lambda: stage_b(2)}
    prepare_b()
    for r in range(3):
        gathered(r)
        prepare_a(r)
        for n in range(20):
            if n < 8:
                outer_step(n)
            else:
                project_step(r, 2 * (n - 8))
            if (r, n) in events:
                events[r, n]()
        finish(r)

    for c in far:
        c.wait_send()
    b_drain()
    for r in range(3):
        to_z(r, 1).wait_send()
        to_z(r, 2).wait_send()

        to_z(r, 3).wait_send()

        for dy in (1, 2, 3):
            for rest in range(2):
                to_y(r, rest, dy).wait_send()
        for dy in range(4):
            to_core(r, dy).wait_send()


def local(first, second, coverage, matrix, offset):
    seqs, block, chans = first.shape
    a = jnp.transpose(first, (1, 2, 0)).reshape(block * chans, seqs)
    b = jnp.transpose(second, (1, 2, 0)).reshape(block * chans, seqs)
    hbm = pl.BlockSpec(memory_space=pltpu.HBM)
    dma = pltpu.SemaphoreType.DMA
    return pl.pallas_call(
        kernel,
        out_shape=pltpu.VMEM((192, NJ, CZ), BF16),
        in_specs=[hbm] * 5,
        out_specs=pl.BlockSpec(memory_space=pltpu.VMEM),
        scratch_shapes=[
            pltpu.VMEM((3, 2, 4, 4, PART, LANES), BF16),
            pltpu.VMEM((4, 2, ROWS, LANES), BF16),
            pltpu.VMEM((ROWS, LANES), BF16),
            pltpu.VMEM((ROWS, LANES), BF16),
            pltpu.VMEM((ROWS, LANES), BF16),
            pltpu.VMEM((256, 256), jnp.int32),
            pltpu.VMEM((256, 256), jnp.int32),
            pltpu.VMEM((2, 256, LANES), F32),
            pltpu.VMEM((2, 256, LANES), F32),
            pltpu.VMEM((2, SPAN, LANES), F32),
            pltpu.VMEM((1024, CZ), BF16),
            pltpu.VMEM((1, CZ), F32),
            pltpu.VMEM((2, CZ, 512), BF16),
            pltpu.VMEM((256, 256), BF16),
            pltpu.VMEM((CHAN, SPAN, 256), BF16),
            pltpu.VMEM((2, 768, 256), BF16),
            pltpu.VMEM((2, 768, 2048), BF16),
            pltpu.VMEM((NJ, 128), F32),
            pltpu.VMEM((3, NJ // 2, 128), F32),
            pltpu.VMEM((SPAN * STRIDE, CZ), F32),
            dma((6,)),
            dma((4, 4)),
            dma((4, 2, 3)),
            dma((3,)),
            dma((3,)),
            dma((3, 3)),
            dma((3, 3)),
            dma((3, 2, 3)),
            dma((3, 2, 3)),
            dma((3, 4)),
            dma((3, 4)),
        ],
        compiler_params=pltpu.CompilerParams(
            collective_id=0, has_side_effects=True, vmem_limit_bytes=52 * 2**20
        ),
        cost_estimate=pl.CostEstimate(flops=7 * 10**9, bytes_accessed=5 * 10**6, transcendentals=0),
    )(a, b, coverage, matrix, offset.reshape(1, CZ))


def solution(mesh):
    in_specs = (P("seq", ("row", "col"), None), P("seq", ("col", "row"), None), P(), P(), P())
    out_specs = P("row", ("col", "seq"), None)
    return jax.shard_map(local, mesh=mesh, in_specs=in_specs, out_specs=out_specs, check_vma=False)
```
